32 devices in a mesh: holes: 2 (over x), depth: 16 (over z, y, core).
Axes of the slice: x: 2, y: 2, z: 4, core: 2. Of those that a mesh axis runs over, the one named last changes fastest.
Arguments:
- spectra: bfloat16 [288, 262144], P(None, ('holes', 'depth')), parts along dimension 1, may hold values from 0 to 100, as said below
- basis: bfloat16 [288, 256], replicated, may hold values from 0.099609375 to 1
- abundance: bfloat16 [256, 262144], P(None, ('holes', 'depth')), parts along dimension 1, may hold values from 0.049804688 to 1
- support: int32 [256, 2048], P(None, ('holes', 'depth')), parts along dimension 1, may hold values from 0 to 1, as said below
Outputs:
- basis_next: bfloat16 [576, 256], P('holes'), parts along dimension 0
- abundance_next: bfloat16 [256, 262144], P(None, ('holes', 'depth')), parts along dimension 1
The draws below stay inside these ranges and needn't reach their ends.
There are 2 independent parts, one for each index of `holes`. The reference program is written for one: setup_inputs(seed, part) draws one part's arguments, and reference() takes and returns one part's arrays. A program takes and returns all parts, laid end to end along the dimension named above; an argument that names none is the same for every part. Nothing has to cross between parts.
Inputs may be any that keep to these rules, and one draw needn't show every extreme that they name: `support`: every component is allowed in at least one block; block densities vary from block to block. `spectra`: Nonnegative.
All inputs are finite; a program needn't handle non-finite values.
Results may differ from the reference program's by a relative error of at most 0.0016.
Values may be sent and summed in bfloat16 or wider, within the bound.
A program may use at most 128 MiB of HBM per device.

```python
import math
import jax
import jax.numpy as jnp
from jax import lax

B = 288
K = 256
BLOCK = 128
PIX_DEV = 8192
PIXELS = 131072
NBLK = 1024


def draw_spectra(key, part):
    first, second = jax.random.split(key, 2)
    regions = PIXELS // PIX_DEV
    base = jax.random.uniform(first, (B, PIXELS), jnp.float32, 0.0, 1.0)
    region = jnp.exp(jax.random.uniform(second, (B, regions), jnp.float32, jnp.log(0.3), 0.0))
    trend = 1.0 + 2.0 * jnp.arange(regions, dtype=jnp.float32) / max(regions - 1, 1)
    factor = jnp.repeat(region * trend[None, :], PIX_DEV, axis=1)
    return (100.0 / 3.0 * base * factor).astype(jnp.bfloat16)


def draw_support(key, part):
    first, second = jax.random.split(key, 2)
    level = jax.random.randint(first, (1, NBLK), 2, 10)
    draws = jax.random.randint(second, (K, NBLK), 0, 10)
    forced = (jnp.arange(K, dtype=jnp.int32) % NBLK)[:, None] == jnp.arange(NBLK, dtype=jnp.int32)[None, :]
    return jnp.logical_or(draws < level, forced).astype(jnp.int32)


def steps_of(rng, dims, cuts, least, largest):
    loudness = 1.0
    for axis_at, shards_of in cuts:
        heights = jax.random.uniform(jax.random.fold_in(jax.random.fold_in(rng, 6), axis_at), (shards_of,), jnp.float32, least / len(cuts), largest / len(cuts))
        loudness = loudness * jnp.repeat(jnp.exp(heights), dims[axis_at] // shards_of).reshape((-1,) + (1,) * (len(dims) - 1 - axis_at))
    return loudness


def setup_inputs(seed: int = 0, part: int = 0) -> dict:
    key_list = jax.random.split(jax.random.key(seed), 5)
    part_splits = jax.random.split(jax.random.fold_in(key_list[4], part), 5)
    spectra = draw_spectra(jax.random.fold_in(jax.random.fold_in(key_list[4], part), 71), part)
    basis = jnp.clip(jnp.exp(jax.random.uniform(key_list[1], (B, K), jnp.float32, math.log(0.099609375), math.log(1.0))), 0.099609375, 1.0).astype(jnp.bfloat16)
    abundance = jnp.clip(0.049804688 + 0.9501953 * jax.random.uniform(part_splits[2], (K, PIXELS), jnp.float32) ** steps_of(part_splits[2], (K, PIXELS), ((1, 16),), -0.2, 0.2), 0.049804688, 1.0).astype(jnp.bfloat16)
    support = draw_support(jax.random.fold_in(jax.random.fold_in(key_list[4], part), 71), part)
    return {"spectra": spectra, "basis": basis, "abundance": abundance, "support": support}


smooth_weight = 3000.0
sparsity = 100.0


def reference(spectra, basis, abundance, support):
    gram_basis = jnp.dot(basis.T, basis, preferred_element_type=jnp.float32).astype(jnp.bfloat16)
    padded = jnp.pad(abundance, ((0, 0), (1, 1)))
    segments = PIXELS // PIX_DEV

    def segment(index):
        start = (index * PIX_DEV).astype(jnp.int32)
        window = lax.dynamic_slice(padded, (jnp.int32(0), start), (K, PIX_DEV + 2))
        pixels = lax.dynamic_slice(spectra, (jnp.int32(0), start), (B, PIX_DEV))
        mask_part = lax.dynamic_slice(support, (jnp.int32(0), (start // BLOCK).astype(jnp.int32)), (K, PIX_DEV // BLOCK))
        project = jnp.dot(basis.T, pixels, preferred_element_type=jnp.float32)
        center = window[:, 1:-1]
        image = jnp.dot(gram_basis, center, preferred_element_type=jnp.float32)
        centre_f = center.astype(jnp.float32)
        beside = window[:, :-2].astype(jnp.float32) + window[:, 2:].astype(jnp.float32)
        active = jnp.repeat(mask_part.astype(jnp.float32), BLOCK, axis=1)
        value = active * centre_f * (project + smooth_weight * beside) / (image + 2.0 * smooth_weight * centre_f + sparsity)
        return value.astype(jnp.bfloat16)

    pieces = lax.map(segment, jnp.arange(segments, dtype=jnp.int32))
    abundance_next = jnp.moveaxis(pieces, 0, 1).reshape(K, PIXELS)
    cross = jnp.dot(spectra, abundance_next.T, preferred_element_type=jnp.float32)
    gram_abund = jnp.dot(abundance_next, abundance_next.T, preferred_element_type=jnp.float32)
    basis_f = basis.astype(jnp.float32)
    lower = jnp.dot(basis_f, gram_abund, precision=lax.Precision.HIGHEST)
    basis_next = (basis_f * cross / lower).astype(jnp.bfloat16)
    return basis_next, abundance_next
```

```python
import functools

import jax
import jax.numpy as jnp
from jax import lax
from jax.experimental import pallas as pl
from jax.experimental.pallas import tpu as pltpu
from jax.sharding import PartitionSpec as P

BLOCK = 128
TILE = 1024
CHUNK = 256
ROWS = 64
NT = (((1,), (1,)), ((), ()))

smooth_weight = 3000.0
sparsity = 100.0


def dot(a, b):
    return jnp.dot(a, b, preferred_element_type=jnp.float32)


def dot_nt(a, b):
    return lax.dot_general(a, b, NT, preferred_element_type=jnp.float32)


def kernel(
    n, sp_hbm, basis_ref, ab_hbm, sup_ref, bn_ref, an_hbm,
    sp_v, ab_v, an_v, sup_v, bt_v, gb_v, acc, half_in, send_v, recv_v, back_v,
    sp_sem, ab_sem, an_sem, halo_s, halo_r, half_s, half_r, red_s, red_r, gat_s, gat_r, fwd_s, fwd_r,
):
    bands, pixels = sp_hbm.shape
    comps = ab_hbm.shape[0]
    tiles = pixels // TILE
    per = TILE // BLOCK
    chips = n // 2
    owners = min(chips, 8)
    stride = chips // owners
    half = comps // 2
    rows = half // owners
    gram_at = acc.shape[1] - comps

    me = lax.axis_index("depth")
    core = lax.rem(me, 2)
    chip = lax.div(me, 2)
    partner = me + 1 - 2 * core

    def load_ab(t):
        return pltpu.make_async_copy(
            ab_hbm.at[:, pl.ds(pl.multiple_of(t * TILE, TILE), TILE)],
            ab_v.at[:, pl.ds(pl.multiple_of(BLOCK + t * TILE, BLOCK), TILE)],
            ab_sem.at[t],
        )

    def load_sp(t):
        where = pl.ds(pl.multiple_of(t * TILE, TILE), TILE)
        return pltpu.make_async_copy(sp_hbm.at[:, where], sp_v.at[:, where], sp_sem.at[t])

    def store_an(t):
        where = pl.ds(pl.multiple_of(t * TILE, TILE), TILE)
        return pltpu.make_async_copy(an_v.at[:, where], an_hbm.at[:, where], an_sem.at[t])

    load_ab(0).start()
    load_ab(1).start()
    load_sp(1).start()
    for t in range(2, tiles):
        load_ab(t).start()
        load_sp(t).start()
    load_sp(0).start()

    barrier = pltpu.get_barrier_semaphore()
    for off in range(1, n):
        pl.semaphore_signal(
            barrier, inc=1, device_id={"depth": lax.rem(me + off, n)}, device_id_type=pl.DeviceIdType.MESH
        )

    to_right = pltpu.make_async_remote_copy(
        src_ref=ab_hbm.at[:, pixels - BLOCK :], dst_ref=ab_v.at[:, :BLOCK],
        send_sem=halo_s.at[0], recv_sem=halo_r.at[0],
        device_id={"depth": lax.rem(me + 1, n)}, device_id_type=pl.DeviceIdType.MESH,
    )
    to_left = pltpu.make_async_remote_copy(
        src_ref=ab_hbm.at[:, :BLOCK], dst_ref=ab_v.at[:, BLOCK + pixels :],
        send_sem=halo_s.at[1], recv_sem=halo_r.at[1],
        device_id={"depth": lax.rem(me + n - 1, n)}, device_id_type=pl.DeviceIdType.MESH,
    )

    basis = basis_ref[...]
    eye = (
        lax.broadcasted_iota(jnp.int32, (comps, comps), 0) == lax.broadcasted_iota(jnp.int32, (comps, comps), 1)
    ).astype(jnp.bfloat16)
    basis_t = dot_nt(eye, basis).astype(jnp.bfloat16)
    bt_v[...] = basis_t
    gb_v[...] = dot(basis_t, basis).astype(jnp.bfloat16)
    for t in range(tiles):
        sup_v[t] = sup_ref[:, t * per : (t + 1) * per].astype(jnp.float32)
    acc[...] = jnp.zeros_like(acc)

    @pl.when(me == 0)
    def _():
        ab_v[:, :BLOCK] = jnp.zeros((comps, BLOCK), jnp.bfloat16)

    @pl.when(me == n - 1)
    def _():
        ab_v[:, BLOCK + pixels :] = jnp.zeros((comps, BLOCK), jnp.bfloat16)

    load_ab(0).wait()
    load_ab(1).wait()

    def tile(t):
        load_sp(t).wait()
        for c in range(TILE // CHUNK):
            at = pl.multiple_of(t * TILE + c * CHUNK, CHUNK)
            project = dot(bt_v[...], sp_v[:, pl.ds(at, CHUNK)])
            image = dot(gb_v[...], ab_v[:, pl.ds(pl.multiple_of(at + BLOCK, BLOCK), CHUNK)])
            for r in range(0, comps, ROWS):
                wide = ab_v[r : r + ROWS, pl.ds(at, CHUNK + 2 * BLOCK)].astype(jnp.float32)
                width = CHUNK + 2 * BLOCK
                low = pltpu.roll(wide, 1, 1)[:, BLOCK : BLOCK + CHUNK]
                high = pltpu.roll(wide, width - 1, 1)[:, BLOCK : BLOCK + CHUNK]
                centre = wide[:, BLOCK : BLOCK + CHUNK]
                first = c * CHUNK // BLOCK
                active = jnp.concatenate(
                    [
                        jnp.broadcast_to(sup_v[t, r : r + ROWS, k : k + 1], (ROWS, BLOCK))
                        for k in range(first, first + CHUNK // BLOCK)
                    ],
                    axis=1,
                )
                under = image[r : r + ROWS] + (2.0 * smooth_weight * centre + sparsity)
                over = (active * centre) * (project[r : r + ROWS] + smooth_weight * (low + high))
                inv = pl.reciprocal(under, approx=True)
                inv = inv * (2.0 - under * inv)
                an_v[r : r + ROWS, pl.ds(at, CHUNK)] = (over * inv).astype(jnp.bfloat16)
        where = pl.ds(pl.multiple_of(t * TILE, TILE), TILE)
        fresh = an_v[:, where]
        acc[:, :bands] += dot_nt(fresh, sp_v[:, where])
        acc[:, gram_at:] += dot_nt(fresh, fresh)
        store_an(t).start()

    def inner(t, carry):
        load_ab(t + 1).wait()
        tile(t)
        return carry

    pl.semaphore_wait(barrier, n - 1)

    @pl.when(me < n - 1)
    def _():
        to_right.start()

    @pl.when(me > 0)
    def _():
        to_left.start()

    lax.fori_loop(1, tiles - 1, inner, 0)

    @pl.when(me > 0)
    def _():
        to_right.wait_recv()
        to_left.wait_send()

    @pl.when(me < n - 1)
    def _():
        to_left.wait_recv()
        to_right.wait_send()

    def outer(j, carry):
        tile((1 - j) * (tiles - 1))
        return carry

    lax.fori_loop(0, 2, outer, 0)

    mine = pl.multiple_of(core * half, half)
    theirs = pl.multiple_of((1 - core) * half, half)
    swap = pltpu.make_async_remote_copy(
        src_ref=acc.at[pl.ds(theirs, half)], dst_ref=half_in,
        send_sem=half_s, recv_sem=half_r,
        device_id={"depth": partner}, device_id_type=pl.DeviceIdType.MESH,
    )
    swap.start()
    swap.wait()
    summed = acc[pl.ds(mine, half), :] + half_in[...]
    half_in[...] = summed
    def split(x):
        high = x.astype(jnp.bfloat16)
        return high, x - high.astype(jnp.float32)

    whole = bands // BLOCK * BLOCK
    tail = bands - whole
    high, low = split(summed[:, :whole])
    tail_high, tail_low = split(summed[:, whole:gram_at])
    send_v[:, :comps] = summed[:, gram_at:].astype(jnp.bfloat16)
    send_v[:, comps : comps + whole] = high
    send_v[:, comps + whole : comps + 2 * whole] = low.astype(jnp.bfloat16)
    send_v[:, comps + 2 * whole :] = (tail_high.astype(jnp.float32) + pltpu.roll(tail_low, tail, 1)).astype(jnp.bfloat16)

    owner = lax.rem(chip, stride) == 0
    home = lax.div(chip, stride)

    def give(off):
        w = lax.rem(home + off, owners)
        return w * stride, pltpu.make_async_remote_copy(
            src_ref=send_v.at[pl.ds(pl.multiple_of(w * rows, rows), rows)], dst_ref=recv_v.at[chip],
            send_sem=red_s.at[off], recv_sem=red_r.at[chip],
            device_id={"depth": 2 * w * stride + core}, device_id_type=pl.DeviceIdType.MESH,
        )

    def take(s):
        return pltpu.make_async_remote_copy(
            src_ref=send_v.at[pl.ds(0, rows)], dst_ref=recv_v.at[s],
            send_sem=red_s.at[0], recv_sem=red_r.at[s],
            device_id={"depth": partner}, device_id_type=pl.DeviceIdType.MESH,
        )

    for off in range(owners):
        dest, copy = give(off)
        pl.when(dest != chip)(copy.start)

    my_row = pl.multiple_of(home * rows, rows)
    out_row = pl.multiple_of(mine + my_row, rows)

    def spread(off, at, src):
        return pltpu.make_async_remote_copy(
            src_ref=back_v.at[pl.ds(at, rows)], dst_ref=back_v.at[pl.ds(at, rows)],
            send_sem=gat_s.at[off], recv_sem=gat_r.at[src],
            device_id={"depth": 2 * lax.rem(chip + off, chips) + core}, device_id_type=pl.DeviceIdType.MESH,
        )

    @pl.when(owner)
    def _():
        recv_v[chip] = jnp.zeros(recv_v.shape[1:], recv_v.dtype)
        for s in range(chips):
            pl.when(s != chip)(take(s).wait_recv)
        own = half_in[pl.ds(my_row, rows), :]
        total = recv_v[0].astype(jnp.float32)
        for s in range(1, chips):
            total = total + recv_v[s].astype(jnp.float32)
        gram_high, gram_low = split(own[:, gram_at:] + total[:, :comps])
        lower = dot(gram_high, bt_v[...]) + dot(gram_low.astype(jnp.bfloat16), bt_v[...])
        ends = total[:, comps + 2 * whole :]
        ends = ends + pltpu.roll(ends, BLOCK - tail, 1)
        middle = total[:, comps : comps + whole] + total[:, comps + whole : comps + 2 * whole]
        cross = own[:, :bands] + jnp.concatenate([middle, ends], axis=1)[:, :bands]
        mine_t = bt_v[pl.ds(out_row, rows), :].astype(jnp.float32)
        back_v[pl.ds(out_row, rows), :bands] = (mine_t * cross / lower).astype(jnp.bfloat16)
        for off in range(1, chips):
            spread(off, out_row, home).start()

    for w in range(owners):
        at = pl.multiple_of(mine + w * rows, rows)
        pl.when(chip != w * stride)(spread(0, at, w).wait_recv)

    forward = pltpu.make_async_remote_copy(
        src_ref=back_v.at[pl.ds(mine, half)], dst_ref=back_v.at[pl.ds(mine, half)],
        send_sem=fwd_s, recv_sem=fwd_r,
        device_id={"depth": partner}, device_id_type=pl.DeviceIdType.MESH,
    )
    forward.start()

    for off in range(owners):
        dest, copy = give(off)
        pl.when(dest != chip)(copy.wait_send)

    @pl.when(owner)
    def _():
        for off in range(1, chips):
            spread(off, out_row, home).wait_send()

    for t in range(tiles):
        store_an(t).wait()
    forward.wait()
    bn_ref[...] = back_v[:, :bands]


def local(spectra, basis, abundance, support):
    n = lax.axis_size("depth")
    bands, pixels = spectra.shape
    comps = abundance.shape[0]
    chips = n // 2
    owners = min(chips, 8)
    tiles = pixels // TILE
    padded = -(-bands // BLOCK) * BLOCK
    lanes = padded + comps
    sent = comps + 2 * (bands // BLOCK * BLOCK) + BLOCK
    half = comps // 2
    dma = pltpu.SemaphoreType.DMA
    macs = comps * (2 * bands + 2 * comps) * pixels
    bn_t, abundance_next = pl.pallas_call(
        functools.partial(kernel, n),
        out_shape=(
            jax.ShapeDtypeStruct((comps, bands), jnp.bfloat16),
            jax.ShapeDtypeStruct((comps, pixels), jnp.bfloat16),
        ),
        in_specs=[
            pl.BlockSpec(memory_space=pl.ANY),
            pl.BlockSpec(memory_space=pltpu.VMEM),
            pl.BlockSpec(memory_space=pl.ANY),
            pl.BlockSpec(memory_space=pltpu.VMEM),
        ],
        out_specs=(pl.BlockSpec(memory_space=pltpu.VMEM), pl.BlockSpec(memory_space=pl.ANY)),
        scratch_shapes=[
            pltpu.VMEM((bands, pixels), jnp.bfloat16),
            pltpu.VMEM((comps, pixels + 2 * BLOCK), jnp.bfloat16),
            pltpu.VMEM((comps, pixels), jnp.bfloat16),
            pltpu.VMEM((tiles, comps, TILE // BLOCK), jnp.float32),
            pltpu.VMEM((comps, bands), jnp.bfloat16),
            pltpu.VMEM((comps, comps), jnp.bfloat16),
            pltpu.VMEM((comps, lanes), jnp.float32),
            pltpu.VMEM((half, lanes), jnp.float32),
            pltpu.VMEM((half, sent), jnp.bfloat16),
            pltpu.VMEM((chips, half // owners, sent), jnp.bfloat16),
            pltpu.VMEM((comps, padded), jnp.bfloat16),
            dma((tiles,)), dma((tiles,)), dma((tiles,)),
            dma((2,)), dma((2,)), dma, dma,
            dma((owners,)), dma((chips,)),
            dma((chips,)), dma((owners,)),
            dma, dma,
        ],
        compiler_params=pltpu.CompilerParams(
            collective_id=0, has_side_effects=True, vmem_limit_bytes=48 * 1024 * 1024
        ),
        cost_estimate=pl.CostEstimate(
            flops=2 * macs, bytes_accessed=2 * pixels * (bands + 2 * comps), transcendentals=0
        ),
    )(spectra, basis, abundance, support)
    return bn_t.T, abundance_next


def solution(mesh):
    placed = (
        P(None, ("holes", "depth")),
        P(),
        P(None, ("holes", "depth")),
        P(None, ("holes", "depth")),
    )
    return jax.shard_map(
        local,
        mesh=mesh,
        in_specs=placed,
        out_specs=(P("holes", None), P(None, ("holes", "depth"))),
        check_vma=False,
    )
```

```python
import functools

import jax
import jax.numpy as jnp
from jax import lax
from jax.experimental import pallas as pl
from jax.experimental.pallas import tpu as pltpu
from jax.sharding import PartitionSpec as P

BLOCK = 128
TILE = 1024
CHUNK = 256
ROWS = 64
PIECES = 8
NT = (((1,), (1,)), ((), ()))

smooth_weight = 3000.0
sparsity = 100.0


def dot(a, b):
    return jnp.dot(a, b, preferred_element_type=jnp.float32)


def dot_nt(a, b):
    return lax.dot_general(a, b, NT, preferred_element_type=jnp.float32)


def kernel(
    n, sp_hbm, basis_hbm, ab_hbm, sup_hbm, bn_ref, an_hbm,
    sp_v, ab_v, an_v, basis_v, flags_v, sup_v, bt_v, gb_v, acc, half_in, send_v, recv_v, back_v,
    small_sem, sp_sem, ab_sem, an_sem, halo_s, halo_r, half_s, half_r, red_s, red_r, gat_s, gat_r,
):
    bands, pixels = sp_hbm.shape
    comps = ab_hbm.shape[0]
    tiles = pixels // TILE
    per = TILE // BLOCK
    chips = n // 2
    owners = min(chips, 8)
    stride = chips // owners
    half = comps // 2
    rows = half // owners
    gram_at = acc.shape[1] - comps

    me = lax.axis_index("depth")
    core = lax.rem(me, 2)
    chip = lax.div(me, 2)
    partner = me + 1 - 2 * core

    def load_ab(t):
        return pltpu.make_async_copy(
            ab_hbm.at[:, pl.ds(pl.multiple_of(t * TILE, TILE), TILE)],
            ab_v.at[:, pl.ds(pl.multiple_of(BLOCK + t * TILE, BLOCK), TILE)],
            ab_sem.at[t],
        )

    def load_sp(t):
        where = pl.ds(pl.multiple_of(t * TILE, TILE), TILE)
        return pltpu.make_async_copy(sp_hbm.at[:, where], sp_v.at[:, where], sp_sem.at[t])

    def store_an(t):
        where = pl.ds(pl.multiple_of(t * TILE, TILE), TILE)
        return pltpu.make_async_copy(an_v.at[:, where], an_hbm.at[:, where], an_sem.at[t])

    load_basis = pltpu.make_async_copy(basis_hbm, basis_v, small_sem.at[0])
    load_flags = pltpu.make_async_copy(sup_hbm, flags_v, small_sem.at[1])
    load_basis.start()
    load_flags.start()
    load_ab(0).start()
    load_ab(1).start()
    load_sp(1).start()
    for t in range(2, tiles):
        load_ab(t).start()
        load_sp(t).start()
    load_sp(0).start()

    barrier = pltpu.get_barrier_semaphore()
    for off in range(1, n):
        pl.semaphore_signal(
            barrier, inc=1, device_id={"depth": lax.rem(me + off, n)}, device_id_type=pl.DeviceIdType.MESH
        )

    to_right = pltpu.make_async_remote_copy(
        src_ref=ab_hbm.at[:, pixels - BLOCK :], dst_ref=ab_v.at[:, :BLOCK],
        send_sem=halo_s.at[0], recv_sem=halo_r.at[0],
        device_id={"depth": lax.rem(me + 1, n)}, device_id_type=pl.DeviceIdType.MESH,
    )
    to_left = pltpu.make_async_remote_copy(
        src_ref=ab_hbm.at[:, :BLOCK], dst_ref=ab_v.at[:, BLOCK + pixels :],
        send_sem=halo_s.at[1], recv_sem=halo_r.at[1],
        device_id={"depth": lax.rem(me + n - 1, n)}, device_id_type=pl.DeviceIdType.MESH,
    )

    acc[...] = jnp.zeros_like(acc)
    load_basis.wait()
    basis = basis_v[...]
    eye = (
        lax.broadcasted_iota(jnp.int32, (comps, comps), 0) == lax.broadcasted_iota(jnp.int32, (comps, comps), 1)
    ).astype(jnp.bfloat16)
    basis_t = dot_nt(eye, basis).astype(jnp.bfloat16)
    bt_v[...] = basis_t
    gb_v[...] = dot(basis_t, basis).astype(jnp.bfloat16)
    load_flags.wait()
    flags = dot_nt(eye, flags_v[...].astype(jnp.float32).astype(jnp.bfloat16))
    for t in range(tiles):
        sup_v[t] = flags[:, t * per : (t + 1) * per]

    @pl.when(me == 0)
    def _():
        ab_v[:, :BLOCK] = jnp.zeros((comps, BLOCK), jnp.bfloat16)

    @pl.when(me == n - 1)
    def _():
        ab_v[:, BLOCK + pixels :] = jnp.zeros((comps, BLOCK), jnp.bfloat16)

    load_ab(0).wait()
    load_ab(1).wait()

    def tile(t):
        load_sp(t).wait()
        for c in range(TILE // CHUNK):
            at = pl.multiple_of(t * TILE + c * CHUNK, CHUNK)
            project = dot(bt_v[...], sp_v[:, pl.ds(at, CHUNK)])
            image = dot(gb_v[...], ab_v[:, pl.ds(pl.multiple_of(at + BLOCK, BLOCK), CHUNK)])
            for r in range(0, comps, ROWS):
                wide = ab_v[r : r + ROWS, pl.ds(at, CHUNK + 2 * BLOCK)].astype(jnp.float32)
                width = CHUNK + 2 * BLOCK
                low = pltpu.roll(wide, 1, 1)[:, BLOCK : BLOCK + CHUNK]
                high = pltpu.roll(wide, width - 1, 1)[:, BLOCK : BLOCK + CHUNK]
                centre = wide[:, BLOCK : BLOCK + CHUNK]
                first = c * CHUNK // BLOCK
                active = jnp.concatenate(
                    [
                        jnp.broadcast_to(sup_v[t, r : r + ROWS, k : k + 1], (ROWS, BLOCK))
                        for k in range(first, first + CHUNK // BLOCK)
                    ],
                    axis=1,
                )
                under = image[r : r + ROWS] + (2.0 * smooth_weight * centre + sparsity)
                over = (active * centre) * (project[r : r + ROWS] + smooth_weight * (low + high))
                inv = pl.reciprocal(under, approx=True)
                inv = inv * (2.0 - under * inv)
                an_v[r : r + ROWS, pl.ds(at, CHUNK)] = (over * inv).astype(jnp.bfloat16)
        where = pl.ds(pl.multiple_of(t * TILE, TILE), TILE)
        fresh = an_v[:, where]
        acc[:, :bands] += dot_nt(fresh, sp_v[:, where])
        acc[:, gram_at:] += dot_nt(fresh, fresh)
        store_an(t).start()

    def inner(t, carry):
        load_ab(t + 1).wait()
        tile(t)
        return carry

    pl.semaphore_wait(barrier, n - 1)

    @pl.when(me < n - 1)
    def _():
        to_right.start()

    @pl.when(me > 0)
    def _():
        to_left.start()

    lax.fori_loop(1, tiles - 1, inner, 0)

    @pl.when(me > 0)
    def _():
        to_right.wait_recv()
        to_left.wait_send()

    @pl.when(me < n - 1)
    def _():
        to_left.wait_recv()
        to_right.wait_send()

    def outer(j, carry):
        tile((1 - j) * (tiles - 1))
        return carry

    lax.fori_loop(0, 2, outer, 0)

    mine = pl.multiple_of(core * half, half)
    theirs = pl.multiple_of((1 - core) * half, half)
    swap = pltpu.make_async_remote_copy(
        src_ref=acc.at[pl.ds(theirs, half)], dst_ref=half_in,
        send_sem=half_s, recv_sem=half_r,
        device_id={"depth": partner}, device_id_type=pl.DeviceIdType.MESH,
    )
    swap.start()
    swap.wait()
    summed = acc[pl.ds(mine, half), :] + half_in[...]
    half_in[...] = summed
    def split(x):
        high = x.astype(jnp.bfloat16)
        return high, x - high.astype(jnp.float32)

    whole = bands // BLOCK * BLOCK
    tail = bands - whole
    high, low = split(summed[:, :whole])
    tail_high, tail_low = split(summed[:, whole:gram_at])
    send_v[:, :comps] = summed[:, gram_at:].astype(jnp.bfloat16)
    send_v[:, comps : comps + whole] = high
    send_v[:, comps + whole : comps + 2 * whole] = low.astype(jnp.bfloat16)
    send_v[:, comps + 2 * whole :] = (tail_high.astype(jnp.float32) + pltpu.roll(tail_low, tail, 1)).astype(jnp.bfloat16)

    owner = lax.rem(chip, stride) == 0
    home = lax.div(chip, stride)

    def give(off):
        w = lax.rem(home + off, owners)
        return w * stride, pltpu.make_async_remote_copy(
            src_ref=send_v.at[pl.ds(pl.multiple_of(w * rows, rows), rows)], dst_ref=recv_v.at[chip],
            send_sem=red_s.at[off], recv_sem=red_r.at[chip],
            device_id={"depth": 2 * w * stride + core}, device_id_type=pl.DeviceIdType.MESH,
        )

    def take(s):
        return pltpu.make_async_remote_copy(
            src_ref=send_v.at[pl.ds(0, rows)], dst_ref=recv_v.at[s],
            send_sem=red_s.at[0], recv_sem=red_r.at[s],
            device_id={"depth": partner}, device_id_type=pl.DeviceIdType.MESH,
        )

    for off in range(owners):
        dest, copy = give(off)
        pl.when(dest != chip)(copy.start)

    my_row = pl.multiple_of(home * rows, rows)
    out_row = pl.multiple_of(mine + my_row, rows)

    def spread(off, at):
        return pltpu.make_async_remote_copy(
            src_ref=back_v.at[pl.ds(at, rows)], dst_ref=back_v.at[pl.ds(at, rows)],
            send_sem=gat_s.at[off], recv_sem=gat_r.at[lax.div(at, rows)],
            device_id={"depth": lax.rem(me + off, n)}, device_id_type=pl.DeviceIdType.MESH,
        )

    @pl.when(owner)
    def _():
        recv_v[chip] = jnp.zeros(recv_v.shape[1:], recv_v.dtype)
        for s in range(chips):
            pl.when(s != chip)(take(s).wait_recv)
        own = half_in[pl.ds(my_row, rows), :]
        total = recv_v[0].astype(jnp.float32)
        for s in range(1, chips):
            total = total + recv_v[s].astype(jnp.float32)
        gram_high, gram_low = split(own[:, gram_at:] + total[:, :comps])
        lower = dot(gram_high, bt_v[...]) + dot(gram_low.astype(jnp.bfloat16), bt_v[...])
        ends = total[:, comps + 2 * whole :]
        ends = ends + pltpu.roll(ends, BLOCK - tail, 1)
        middle = total[:, comps : comps + whole] + total[:, comps + whole : comps + 2 * whole]
        cross = own[:, :bands] + jnp.concatenate([middle, ends], axis=1)[:, :bands]
        mine_t = bt_v[pl.ds(out_row, rows), :].astype(jnp.float32)
        back_v[pl.ds(out_row, rows), :bands] = (mine_t * cross / lower).astype(jnp.bfloat16)
        for off in range(1, n):
            spread(off, out_row).start()

    for off in range(owners):
        dest, copy = give(off)
        pl.when(dest != chip)(copy.wait_send)

    @pl.when(owner)
    def _():
        for off in range(1, n):
            spread(off, out_row).wait_send()

    for t in range(tiles):
        store_an(t).wait()
    for w in range(2 * owners):
        at = w * rows
        source = 2 * (w % owners) * stride + w // owners
        pl.when(me != source)(spread(0, at).wait_recv)
    bn_ref[...] = back_v[:, :bands]


def settle(bn_t_ref, an_in, bn_ref, an_out, sem):
    comps = an_in.shape[0]
    rows = comps // PIECES
    copies = [
        pltpu.make_async_copy(an_in.at[pl.ds(i * rows, rows)], an_out.at[pl.ds(i * rows, rows)], sem.at[i])
        for i in range(PIECES)
    ]
    for copy in copies:
        copy.start()
    eye = (
        lax.broadcasted_iota(jnp.int32, (comps, comps), 0) == lax.broadcasted_iota(jnp.int32, (comps, comps), 1)
    ).astype(jnp.bfloat16)
    bn_ref[...] = lax.dot_general(
        bn_t_ref[...], eye, (((0,), (0,)), ((), ())), preferred_element_type=jnp.float32
    ).astype(jnp.bfloat16)
    for copy in copies:
        copy.wait()


def local(spectra, basis, abundance, support):
    n = lax.axis_size("depth")
    bands, pixels = spectra.shape
    comps = abundance.shape[0]
    chips = n // 2
    owners = min(chips, 8)
    tiles = pixels // TILE
    padded = -(-bands // BLOCK) * BLOCK
    lanes = padded + comps
    sent = comps + 2 * (bands // BLOCK * BLOCK) + BLOCK
    half = comps // 2
    dma = pltpu.SemaphoreType.DMA
    macs = comps * (2 * bands + 2 * comps) * pixels
    bn_t, abundance_next = pl.pallas_call(
        functools.partial(kernel, n),
        out_shape=(
            jax.ShapeDtypeStruct((comps, bands), jnp.bfloat16),
            jax.ShapeDtypeStruct((comps, pixels), jnp.bfloat16),
        ),
        in_specs=[
            pl.BlockSpec(memory_space=pl.ANY),
            pl.BlockSpec(memory_space=pltpu.HBM),
            pl.BlockSpec(memory_space=pl.ANY),
            pl.BlockSpec(memory_space=pltpu.HBM),
        ],
        out_specs=(pl.BlockSpec(memory_space=pltpu.VMEM), pl.BlockSpec(memory_space=pl.ANY)),
        scratch_shapes=[
            pltpu.VMEM((bands, pixels), jnp.bfloat16),
            pltpu.VMEM((comps, pixels + 2 * BLOCK), jnp.bfloat16),
            pltpu.VMEM((comps, pixels), jnp.bfloat16),
            pltpu.VMEM(basis.shape, jnp.bfloat16),
            pltpu.VMEM(support.shape[::-1], jnp.int32),
            pltpu.VMEM((tiles, comps, TILE // BLOCK), jnp.float32),
            pltpu.VMEM((comps, bands), jnp.bfloat16),
            pltpu.VMEM((comps, comps), jnp.bfloat16),
            pltpu.VMEM((comps, lanes), jnp.float32),
            pltpu.VMEM((half, lanes), jnp.float32),
            pltpu.VMEM((half, sent), jnp.bfloat16),
            pltpu.VMEM((chips, half // owners, sent), jnp.bfloat16),
            pltpu.VMEM((comps, padded), jnp.bfloat16),
            dma((2,)), dma((tiles,)), dma((tiles,)), dma((tiles,)),
            dma((2,)), dma((2,)), dma, dma,
            dma((owners,)), dma((chips,)),
            dma((n,)), dma((2 * owners,)),
        ],
        compiler_params=pltpu.CompilerParams(
            collective_id=0, has_side_effects=True, vmem_limit_bytes=48 * 1024 * 1024
        ),
        cost_estimate=pl.CostEstimate(
            flops=2 * macs, bytes_accessed=2 * pixels * (bands + 2 * comps), transcendentals=0
        ),
    )(spectra, basis, abundance, support.T)
    return pl.pallas_call(
        settle,
        out_shape=(
            jax.ShapeDtypeStruct((bands, comps), jnp.bfloat16),
            jax.ShapeDtypeStruct((comps, pixels), jnp.bfloat16),
        ),
        in_specs=[pl.BlockSpec(memory_space=pltpu.VMEM), pl.BlockSpec(memory_space=pl.ANY)],
        out_specs=(pl.BlockSpec(memory_space=pltpu.VMEM), pl.BlockSpec(memory_space=pl.ANY)),
        scratch_shapes=[dma((PIECES,))],
        compiler_params=pltpu.CompilerParams(vmem_limit_bytes=4 * 1024 * 1024),
    )(bn_t, abundance_next)


def solution(mesh):
    placed = (
        P(None, ("holes", "depth")),
        P(),
        P(None, ("holes", "depth")),
        P(None, ("holes", "depth")),
    )
    return jax.shard_map(
        local,
        mesh=mesh,
        in_specs=placed,
        out_specs=(P("holes", None), P(None, ("holes", "depth"))),
        check_vma=False,
    )
```

```python
import functools

import jax
import jax.numpy as jnp
from jax import lax
from jax.experimental import pallas as pl
from jax.experimental.pallas import tpu as pltpu
from jax.sharding import PartitionSpec as P

BLOCK = 128
TILE = 2048
CHUNK = 512
ROWS = 64
PIECES = 8
NT = (((1,), (1,)), ((), ()))

smooth_weight = 3000.0
sparsity = 100.0


def dot(a, b):
    return jnp.dot(a, b, preferred_element_type=jnp.float32)


def dot_nt(a, b):
    return lax.dot_general(a, b, NT, preferred_element_type=jnp.float32)


def kernel(
    n, sp_hbm, basis_hbm, ab_hbm, sup_hbm, bn_ref, an_hbm,
    sp_v, ab_v, an_v, basis_v, flags_v, sup_v, bt_v, gb_v, acc, half_in, send_v, recv_v, back_v,
    small_sem, sp_sem, ab_sem, an_sem, halo_s, halo_r, half_s, half_r, red_s, red_r, gat_s, gat_r,
):
    bands, pixels = sp_hbm.shape
    comps = ab_hbm.shape[0]
    tiles = pixels // TILE
    per = TILE // BLOCK
    chips = n // 2
    owners = min(chips, 8)
    stride = chips // owners
    half = comps // 2
    rows = half // owners
    gram_at = acc.shape[1] - comps

    me = lax.axis_index("depth")
    core = lax.rem(me, 2)
    chip = lax.div(me, 2)
    partner = me + 1 - 2 * core

    def load_ab(t):
        return pltpu.make_async_copy(
            ab_hbm.at[:, pl.ds(pl.multiple_of(t * TILE, TILE), TILE)],
            ab_v.at[:, pl.ds(pl.multiple_of(BLOCK + t * TILE, BLOCK), TILE)],
            ab_sem.at[t],
        )

    def load_sp(t):
        where = pl.ds(pl.multiple_of(t * TILE, TILE), TILE)
        return pltpu.make_async_copy(sp_hbm.at[:, where], sp_v.at[:, where], sp_sem.at[t])

    def store_an(t):
        where = pl.ds(pl.multiple_of(t * TILE, TILE), TILE)
        return pltpu.make_async_copy(an_v.at[:, where], an_hbm.at[:, where], an_sem.at[t])

    load_basis = pltpu.make_async_copy(basis_hbm, basis_v, small_sem.at[0])
    load_flags = pltpu.make_async_copy(sup_hbm, flags_v, small_sem.at[1])
    load_basis.start()
    load_flags.start()
    load_ab(0).start()
    load_ab(1).start()
    load_sp(1).start()
    for t in range(2, tiles):
        load_ab(t).start()
        load_sp(t).start()
    load_sp(0).start()

    barrier = pltpu.get_barrier_semaphore()
    for off in range(1, n):
        pl.semaphore_signal(
            barrier, inc=1, device_id={"depth": lax.rem(me + off, n)}, device_id_type=pl.DeviceIdType.MESH
        )

    to_right = pltpu.make_async_remote_copy(
        src_ref=ab_hbm.at[:, pixels - BLOCK :], dst_ref=ab_v.at[:, :BLOCK],
        send_sem=halo_s.at[0], recv_sem=halo_r.at[0],
        device_id={"depth": lax.rem(me + 1, n)}, device_id_type=pl.DeviceIdType.MESH,
    )
    to_left = pltpu.make_async_remote_copy(
        src_ref=ab_hbm.at[:, :BLOCK], dst_ref=ab_v.at[:, BLOCK + pixels :],
        send_sem=halo_s.at[1], recv_sem=halo_r.at[1],
        device_id={"depth": lax.rem(me + n - 1, n)}, device_id_type=pl.DeviceIdType.MESH,
    )

    acc[...] = jnp.zeros_like(acc)
    load_basis.wait()
    basis = basis_v[...]
    eye = (
        lax.broadcasted_iota(jnp.int32, (comps, comps), 0) == lax.broadcasted_iota(jnp.int32, (comps, comps), 1)
    ).astype(jnp.bfloat16)
    basis_t = dot_nt(eye, basis).astype(jnp.bfloat16)
    bt_v[...] = basis_t
    gb_v[...] = dot(basis_t, basis).astype(jnp.bfloat16)
    load_flags.wait()
    flags = dot_nt(eye, flags_v[...].astype(jnp.float32).astype(jnp.bfloat16))
    for t in range(tiles):
        sup_v[t] = flags[:, t * per : (t + 1) * per]

    @pl.when(me == 0)
    def _():
        ab_v[:, :BLOCK] = jnp.zeros((comps, BLOCK), jnp.bfloat16)

    @pl.when(me == n - 1)
    def _():
        ab_v[:, BLOCK + pixels :] = jnp.zeros((comps, BLOCK), jnp.bfloat16)

    load_ab(0).wait()
    load_ab(1).wait()

    def tile(t):
        load_sp(t).wait()
        for c in range(TILE // CHUNK):
            at = pl.multiple_of(t * TILE + c * CHUNK, CHUNK)
            project = dot(bt_v[...], sp_v[:, pl.ds(at, CHUNK)])
            image = dot(gb_v[...], ab_v[:, pl.ds(pl.multiple_of(at + BLOCK, BLOCK), CHUNK)])
            for r in range(0, comps, ROWS):
                wide = ab_v[r : r + ROWS, pl.ds(at, CHUNK + 2 * BLOCK)].astype(jnp.float32)
                width = CHUNK + 2 * BLOCK
                low = pltpu.roll(wide, 1, 1)[:, BLOCK : BLOCK + CHUNK]
                high = pltpu.roll(wide, width - 1, 1)[:, BLOCK : BLOCK + CHUNK]
                centre = wide[:, BLOCK : BLOCK + CHUNK]
                first = c * CHUNK // BLOCK
                active = jnp.concatenate(
                    [
                        jnp.broadcast_to(sup_v[t, r : r + ROWS, k : k + 1], (ROWS, BLOCK))
                        for k in range(first, first + CHUNK // BLOCK)
                    ],
                    axis=1,
                )
                under = image[r : r + ROWS] + (2.0 * smooth_weight * centre + sparsity)
                over = (active * centre) * (project[r : r + ROWS] + smooth_weight * (low + high))
                inv = pl.reciprocal(under, approx=True)
                inv = inv * (2.0 - under * inv)
                an_v[r : r + ROWS, pl.ds(at, CHUNK)] = (over * inv).astype(jnp.bfloat16)
        where = pl.ds(pl.multiple_of(t * TILE, TILE), TILE)
        fresh = an_v[:, where]
        acc[:, :bands] += dot_nt(fresh, sp_v[:, where])
        acc[:, gram_at:] += dot_nt(fresh, fresh)
        store_an(t).start()

    def inner(t, carry):
        load_ab(t + 1).wait()
        tile(t)
        return carry

    pl.semaphore_wait(barrier, n - 1)

    @pl.when(me < n - 1)
    def _():
        to_right.start()

    @pl.when(me > 0)
    def _():
        to_left.start()

    lax.fori_loop(1, tiles - 1, inner, 0)

    @pl.when(me > 0)
    def _():
        to_right.wait_recv()
        to_left.wait_send()

    @pl.when(me < n - 1)
    def _():
        to_left.wait_recv()
        to_right.wait_send()

    def outer(j, carry):
        tile((1 - j) * (tiles - 1))
        return carry

    lax.fori_loop(0, 2, outer, 0)

    mine = pl.multiple_of(core * half, half)
    theirs = pl.multiple_of((1 - core) * half, half)
    swap = pltpu.make_async_remote_copy(
        src_ref=acc.at[pl.ds(theirs, half)], dst_ref=half_in,
        send_sem=half_s, recv_sem=half_r,
        device_id={"depth": partner}, device_id_type=pl.DeviceIdType.MESH,
    )
    swap.start()
    swap.wait()
    summed = acc[pl.ds(mine, half), :] + half_in[...]
    half_in[...] = summed
    def split(x):
        high = x.astype(jnp.bfloat16)
        return high, x - high.astype(jnp.float32)

    whole = bands // BLOCK * BLOCK
    tail = bands - whole
    high, low = split(summed[:, :whole])
    tail_high, tail_low = split(summed[:, whole:gram_at])
    send_v[:, :comps] = summed[:, gram_at:].astype(jnp.bfloat16)
    send_v[:, comps : comps + whole] = high
    send_v[:, comps + whole : comps + 2 * whole] = low.astype(jnp.bfloat16)
    send_v[:, comps + 2 * whole :] = (tail_high.astype(jnp.float32) + pltpu.roll(tail_low, tail, 1)).astype(jnp.bfloat16)

    owner = lax.rem(chip, stride) == 0
    home = lax.div(chip, stride)

    def give(off):
        w = lax.rem(home + off, owners)
        return w * stride, pltpu.make_async_remote_copy(
            src_ref=send_v.at[pl.ds(pl.multiple_of(w * rows, rows), rows)], dst_ref=recv_v.at[chip],
            send_sem=red_s.at[off], recv_sem=red_r.at[chip],
            device_id={"depth": 2 * w * stride + core}, device_id_type=pl.DeviceIdType.MESH,
        )

    def take(s):
        return pltpu.make_async_remote_copy(
            src_ref=send_v.at[pl.ds(0, rows)], dst_ref=recv_v.at[s],
            send_sem=red_s.at[0], recv_sem=red_r.at[s],
            device_id={"depth": partner}, device_id_type=pl.DeviceIdType.MESH,
        )

    for off in range(owners):
        dest, copy = give(off)
        pl.when(dest != chip)(copy.start)

    my_row = pl.multiple_of(home * rows, rows)
    out_row = pl.multiple_of(mine + my_row, rows)

    def spread(off, at):
        return pltpu.make_async_remote_copy(
            src_ref=back_v.at[pl.ds(at, rows)], dst_ref=back_v.at[pl.ds(at, rows)],
            send_sem=gat_s.at[off], recv_sem=gat_r.at[lax.div(at, rows)],
            device_id={"depth": lax.rem(me + off, n)}, device_id_type=pl.DeviceIdType.MESH,
        )

    @pl.when(owner)
    def _():
        recv_v[chip] = jnp.zeros(recv_v.shape[1:], recv_v.dtype)
        for s in range(chips):
            pl.when(s != chip)(take(s).wait_recv)
        own = half_in[pl.ds(my_row, rows), :]
        total = recv_v[0].astype(jnp.float32)
        for s in range(1, chips):
            total = total + recv_v[s].astype(jnp.float32)
        gram_high, gram_low = split(own[:, gram_at:] + total[:, :comps])
        lower = dot(gram_high, bt_v[...]) + dot(gram_low.astype(jnp.bfloat16), bt_v[...])
        ends = total[:, comps + 2 * whole :]
        ends = ends + pltpu.roll(ends, BLOCK - tail, 1)
        middle = total[:, comps : comps + whole] + total[:, comps + whole : comps + 2 * whole]
        cross = own[:, :bands] + jnp.concatenate([middle, ends], axis=1)[:, :bands]
        mine_t = bt_v[pl.ds(out_row, rows), :].astype(jnp.float32)
        back_v[pl.ds(out_row, rows), :bands] = (mine_t * cross / lower).astype(jnp.bfloat16)
        for off in range(1, n):
            spread(off, out_row).start()

    for off in range(owners):
        dest, copy = give(off)
        pl.when(dest != chip)(copy.wait_send)

    @pl.when(owner)
    def _():
        for off in range(1, n):
            spread(off, out_row).wait_send()

    for t in range(tiles):
        store_an(t).wait()
    for w in range(2 * owners):
        at = w * rows
        source = 2 * (w % owners) * stride + w // owners
        pl.when(me != source)(spread(0, at).wait_recv)
    bn_ref[...] = back_v[:, :bands]


def settle(bn_t_ref, an_in, bn_ref, an_out, sem):
    comps = an_in.shape[0]
    rows = comps // PIECES
    copies = [
        pltpu.make_async_copy(an_in.at[pl.ds(i * rows, rows)], an_out.at[pl.ds(i * rows, rows)], sem.at[i])
        for i in range(PIECES)
    ]
    for copy in copies:
        copy.start()
    eye = (
        lax.broadcasted_iota(jnp.int32, (comps, comps), 0) == lax.broadcasted_iota(jnp.int32, (comps, comps), 1)
    ).astype(jnp.bfloat16)
    bn_ref[...] = lax.dot_general(
        bn_t_ref[...], eye, (((0,), (0,)), ((), ())), preferred_element_type=jnp.float32
    ).astype(jnp.bfloat16)
    for copy in copies:
        copy.wait()


def local(spectra, basis, abundance, support):
    n = lax.axis_size("depth")
    bands, pixels = spectra.shape
    comps = abundance.shape[0]
    chips = n // 2
    owners = min(chips, 8)
    tiles = pixels // TILE
    padded = -(-bands // BLOCK) * BLOCK
    lanes = padded + comps
    sent = comps + 2 * (bands // BLOCK * BLOCK) + BLOCK
    half = comps // 2
    dma = pltpu.SemaphoreType.DMA
    macs = comps * (2 * bands + 2 * comps) * pixels
    bn_t, abundance_next = pl.pallas_call(
        functools.partial(kernel, n),
        out_shape=(
            jax.ShapeDtypeStruct((comps, bands), jnp.bfloat16),
            jax.ShapeDtypeStruct((comps, pixels), jnp.bfloat16),
        ),
        in_specs=[
            pl.BlockSpec(memory_space=pl.ANY),
            pl.BlockSpec(memory_space=pltpu.HBM),
            pl.BlockSpec(memory_space=pl.ANY),
            pl.BlockSpec(memory_space=pltpu.HBM),
        ],
        out_specs=(pl.BlockSpec(memory_space=pltpu.VMEM), pl.BlockSpec(memory_space=pl.ANY)),
        scratch_shapes=[
            pltpu.VMEM((bands, pixels), jnp.bfloat16),
            pltpu.VMEM((comps, pixels + 2 * BLOCK), jnp.bfloat16),
            pltpu.VMEM((comps, pixels), jnp.bfloat16),
            pltpu.VMEM(basis.shape, jnp.bfloat16),
            pltpu.VMEM(support.shape[::-1], jnp.int32),
            pltpu.VMEM((tiles, comps, TILE // BLOCK), jnp.float32),
            pltpu.VMEM((comps, bands), jnp.bfloat16),
            pltpu.VMEM((comps, comps), jnp.bfloat16),
            pltpu.VMEM((comps, lanes), jnp.float32),
            pltpu.VMEM((half, lanes), jnp.float32),
            pltpu.VMEM((half, sent), jnp.bfloat16),
            pltpu.VMEM((chips, half // owners, sent), jnp.bfloat16),
            pltpu.VMEM((comps, padded), jnp.bfloat16),
            dma((2,)), dma((tiles,)), dma((tiles,)), dma((tiles,)),
            dma((2,)), dma((2,)), dma, dma,
            dma((owners,)), dma((chips,)),
            dma((n,)), dma((2 * owners,)),
        ],
        compiler_params=pltpu.CompilerParams(
            collective_id=0, has_side_effects=True, vmem_limit_bytes=48 * 1024 * 1024
        ),
        cost_estimate=pl.CostEstimate(
            flops=2 * macs, bytes_accessed=2 * pixels * (bands + 2 * comps), transcendentals=0
        ),
    )(spectra, basis, abundance, support.T)
    return pl.pallas_call(
        settle,
        out_shape=(
            jax.ShapeDtypeStruct((bands, comps), jnp.bfloat16),
            jax.ShapeDtypeStruct((comps, pixels), jnp.bfloat16),
        ),
        in_specs=[pl.BlockSpec(memory_space=pltpu.VMEM), pl.BlockSpec(memory_space=pl.ANY)],
        out_specs=(pl.BlockSpec(memory_space=pltpu.VMEM), pl.BlockSpec(memory_space=pl.ANY)),
        scratch_shapes=[dma((PIECES,))],
        compiler_params=pltpu.CompilerParams(vmem_limit_bytes=4 * 1024 * 1024),
    )(bn_t, abundance_next)


def solution(mesh):
    placed = (
        P(None, ("holes", "depth")),
        P(),
        P(None, ("holes", "depth")),
        P(None, ("holes", "depth")),
    )
    return jax.shard_map(
        local,
        mesh=mesh,
        in_specs=placed,
        out_specs=(P("holes", None), P(None, ("holes", "depth"))),
        check_vma=False,
    )
```
